512 devices in a mesh: tm: 64 (over y, x, core), gz: 8 (over z).
Axes of the slice: x: 4, y: 8, z: 8, core: 2. Of those that a mesh axis runs over, the one named last changes fastest.
Arguments:
- cpoint_guess: float32 [64, 32, 32, 128], P('tm', 'gz'), may hold values from -1 to 1
- initial_state: float32 [32, 32, 128], P('gz'), may hold values from -1 to 1
- diffusivity: float32 [32, 32, 128], P('gz'), may hold values from 0.05 to 1
- growth_rate: float32 [32, 32, 128], P('gz'), may hold values from 0.5 to 2
Outputs:
- corrected: float32 [64, 32, 32, 128], P('tm', 'gz')
- residual: float32 [64, 32, 32, 128], P('tm', 'gz')
The draws below stay inside these ranges and needn't reach their ends.
All inputs are finite; a program needn't handle non-finite values.
Results may differ from the reference program's by a relative error of at most 0.00002.
Values sent between devices are 32-bit elements; how exact they have to be, the bound alone decides.
No kernel may reach another device: no remote copies, remote signals or barrier semaphores. Data moves between devices by JAX's collectives and lax.ppermute only.
A program may use at most 64 MiB of HBM per device.

```python
import math
import jax
import jax.numpy as jnp
from jax import lax

NX = 32
NY = 128
STEPS = 8
INTERVALS = 64
NZ = 32


def block_levels(rng, extent, cuts, low, high):
    level = 1.0
    for axis_at, blocks in cuts:
        heights = jax.random.uniform(jax.random.fold_in(jax.random.fold_in(rng, 6), axis_at), (blocks,), jnp.float32, low / len(cuts), high / len(cuts))
        level = level * jnp.repeat(jnp.exp(heights), extent[axis_at] // blocks).reshape((-1,) + (1,) * (len(extent) - 1 - axis_at))
    return level


def setup_inputs(seed: int = 0) -> dict:
    splits = jax.random.split(jax.random.key(seed), 5)
    return {
        "cpoint_guess": jnp.clip(jax.random.uniform(splits[0], (INTERVALS, NZ, NX, NY), jnp.float32, -1.0, 1.0) * block_levels(splits[0], (INTERVALS, NZ, NX, NY), ((0, 64), (1, 8)), -0.4, 0.0), -1.0, 1.0),
        "initial_state": jnp.clip(jax.random.uniform(splits[1], (NZ, NX, NY), jnp.float32, -1.0, 1.0) * block_levels(splits[1], (NZ, NX, NY), ((0, 8),), -0.4, 0.0), -1.0, 1.0),
        "diffusivity": jnp.clip(jnp.exp(math.log(1.0) - 2.9957323 * jax.random.uniform(splits[2], (NZ, NX, NY), jnp.float32) ** block_levels(splits[2], (NZ, NX, NY), ((0, 8),), -0.2, 0.2)), 0.05, 1.0),
        "growth_rate": jnp.clip(jnp.exp(math.log(2.0) - 1.3862944 * jax.random.uniform(splits[3], (NZ, NX, NY), jnp.float32) ** block_levels(splits[3], (NZ, NX, NY), ((0, 8),), -0.2, 0.2)), 0.5, 2.0),
    }


FINE_STEP = 0.01875


def advance(extended, kappa_ext, growth_mid, time_step):
    center = extended[..., 1:-1, :, :]
    kappa_mid = kappa_ext[..., 1:-1, :, :]
    widths = [(0, 0)] * (center.ndim - 2) + [(1, 1), (1, 1)]
    kappa_widths = [(0, 0)] * (kappa_mid.ndim - 2) + [(1, 1), (1, 1)]
    padded = jnp.pad(center, widths)
    kappa_pad = jnp.pad(kappa_mid, kappa_widths)
    neighbours = [
        (extended[..., 2:, :, :], kappa_ext[..., 2:, :, :]),
        (extended[..., :-2, :, :], kappa_ext[..., :-2, :, :]),
        (padded[..., :, 2:, 1:-1], kappa_pad[..., :, 2:, 1:-1]),
        (padded[..., :, :-2, 1:-1], kappa_pad[..., :, :-2, 1:-1]),
        (padded[..., :, 1:-1, 2:], kappa_pad[..., :, 1:-1, 2:]),
        (padded[..., :, 1:-1, :-2], kappa_pad[..., :, 1:-1, :-2]),
    ]
    flux_sum = jnp.zeros_like(center)
    for values, kappas in neighbours:
        flux_sum = flux_sum + 0.5 * (kappas + kappa_mid) * (values - center)
    reaction = growth_mid * (center - center * center * center)
    return center + time_step * (flux_sum + reaction)


def pad_depth(states):
    return jnp.pad(states, [(0, 0)] * (states.ndim - 3) + [(1, 1), (0, 0), (0, 0)])


def reference(cpoint_guess, initial_state, diffusivity, growth_rate):
    kappa_ext = pad_depth(diffusivity)

    def fine_span(states):
        for substep in range(STEPS):
            states = advance(pad_depth(states), kappa_ext, growth_rate, FINE_STEP)
        return states

    def coarse_step(states):
        return advance(pad_depth(states), kappa_ext, growth_rate, FINE_STEP * STEPS)

    opening = jnp.concatenate([initial_state[None], cpoint_guess[:-1]], axis=0)
    relaxed = fine_span(opening)
    restart = jnp.concatenate([initial_state[None], relaxed[:-1]], axis=0)
    reached = fine_span(restart)
    residual = reached - relaxed
    forcing = reached - coarse_step(restart)

    def chain_step(previous, forcing_now):
        following = coarse_step(previous) + forcing_now
        return following, following

    unused, corrected = lax.scan(chain_step, initial_state, forcing)
    return corrected, residual
```

```python
import functools

import jax
import jax.numpy as jnp
from jax import lax
from jax.experimental import pallas as pl
from jax.experimental.pallas import tpu as pltpu
from jax.sharding import PartitionSpec as P

STEPS = 8
FINE_STEP = 0.01875
COARSE_STEP = FINE_STEP * STEPS
NZ, NX, NY = 32, 32, 128
SLAB = 4
HALF = NZ // 2
UNROLL = 4
ROW = 8
VMEM_BYTES = 52 * 1024 * 1024

PLANE = (NX, NY)
PADDED = (NZ + 2, NX + 16, NY)
COEFS = 7


def scratch_set():
    full = pltpu.VMEM((NZ, *PLANE), jnp.float32)
    return [
        pltpu.VMEM(PADDED, jnp.float32),
        pltpu.VMEM(PADDED, jnp.float32),
        pltpu.VMEM((NZ + 1, *PLANE), jnp.float32),
        full,
        full,
        full,
        full,
        full,
        full,
    ]


def put(ref, z, value):
    ref[z + 1, ROW : ROW + NX, :] = value


def get(ref, z):
    return ref[z + 1, ROW : ROW + NX, :]


def clear_edges(ref):
    ref[0] = jnp.zeros(PADDED[1:], jnp.float32)
    ref[NZ + 1] = jnp.zeros(PADDED[1:], jnp.float32)

    def body(z, carry):
        ref[z + 1, 0:ROW, :] = jnp.zeros((ROW, NY), jnp.float32)
        ref[z + 1, ROW + NX : 2 * ROW + NX, :] = jnp.zeros((ROW, NY), jnp.float32)
        return carry

    lax.fori_loop(0, NZ, body, 0)


def build(a, coefs, kappa, growth, h):
    az, axm, axp, aym, ayp, diag, react = coefs
    half_h = 0.5 * h
    for z in range(NZ):
        put(a, z, kappa(z))
    lane = lax.broadcasted_iota(jnp.int32, PLANE, 1)

    az[0] = half_h * get(a, 0)

    def body(z, carry):
        k = get(a, z)
        up = half_h * (a[z + 2, ROW : ROW + NX, :] + k)
        down = half_h * (a[z, ROW : ROW + NX, :] + k)
        xm = half_h * (a[z + 1, ROW - 1 : ROW - 1 + NX, :] + k)
        xp = half_h * (a[z + 1, ROW + 1 : ROW + 1 + NX, :] + k)
        ym = half_h * (jnp.where(lane == 0, 0.0, pltpu.roll(k, 1, 1)) + k)
        yp = half_h * (jnp.where(lane == NY - 1, 0.0, pltpu.roll(k, NY - 1, 1)) + k)
        az[z + 1] = up
        axm[z] = xm
        axp[z] = xp
        aym[z] = jnp.where(lane == 0, 0.0, ym)
        ayp[z] = jnp.where(lane == NY - 1, 0.0, yp)
        hr = react[z]
        diag[z] = 1.0 + hr - (up + down + xm + xp + ym + yp)
        return carry

    for z in range(NZ):
        react[z] = h * growth(z)
    lax.fori_loop(0, NZ, body, 0)


def rescale(coefs, factor):
    def body(z, carry):
        for ref in coefs[:5] + coefs[6:]:
            ref[z] = factor * ref[z]
        coefs[5][z] = 1.0 + factor * (coefs[5][z] - 1.0)
        return carry

    lax.fori_loop(0, NZ, body, 0)
    coefs[0][NZ] = factor * coefs[0][NZ]


def step(src, dst, coefs, finish=None):
    az, axm, axp, aym, ayp, diag, react = coefs

    def chunk(i, carry):
        base = i * UNROLL
        below = src[base, ROW : ROW + NX, :]
        here = src[base + 1, ROW : ROW + NX, :]
        face = az[base]
        for j in range(UNROLL):
            z = base + j
            above = src[z + 2, ROW : ROW + NX, :]
            next_face = az[z + 1]
            value = here * (diag[z] - react[z] * (here * here))
            value = value + (face * below + next_face * above)
            value = value + (
                axm[z] * src[z + 1, ROW - 1 : ROW - 1 + NX, :]
                + axp[z] * src[z + 1, ROW + 1 : ROW + 1 + NX, :]
            )
            value = value + (aym[z] * pltpu.roll(here, 1, 1) + ayp[z] * pltpu.roll(here, NY - 1, 1))
            if finish is not None:
                value = finish(z, value)
            dst[z + 1, ROW : ROW + NX, :] = value
            below, here, face = here, above, next_face
        return carry

    lax.fori_loop(0, NZ // UNROLL, chunk, 0)


def fine(a, b, coefs):
    def pair(i, carry):
        step(a, b, coefs)
        step(b, a, coefs)
        return carry

    lax.fori_loop(0, STEPS // 2, pair, 0)


def copy_slab(src, first, out):
    for i in range(SLAB):
        out[i] = get(src, first + i)


def copy_state(src, dst):
    def body(z, carry):
        put(dst, z, get(src, z))
        return carry

    lax.fori_loop(0, NZ, body, 0)


def copy_out(src, out):
    def body(z, carry):
        out[z] = get(src, z)
        return carry

    lax.fori_loop(0, NZ, body, 0)


def field(gathered, number):
    return lambda z: gathered[z // SLAB, number, z % SLAB]


def fine_kernel(where, gathered, keep, send, u_out, w_out, a, b, *coefs):
    first = where[0] * SLAB
    core = where[1]
    clear_edges(a)
    clear_edges(b)
    build(a, coefs, field(gathered, 1), field(gathered, 2), FINE_STEP)
    for z in range(NZ):
        put(a, z, gathered[z // SLAB, 0, z % SLAB])
    fine(a, b, coefs)
    copy_slab(a, first, u_out)

    def save(z, carry):
        keep[z] = get(a, core * HALF + z)
        send[z] = get(a, (1 - core) * HALF + z)
        return carry

    lax.fori_loop(0, HALF, save, 0)
    fine(a, b, coefs)
    copy_slab(a, first, w_out)

    def restore(z, carry):
        put(b, core * HALF + z, keep[z])
        put(b, (1 - core) * HALF + z, send[z])
        return carry

    lax.fori_loop(0, HALF, restore, 0)
    rescale(coefs, float(STEPS))
    step(b, a, coefs, finish=lambda z, value: get(a, z) - value)

    def emit(z, carry):
        keep[z] = get(a, core * HALF + z)
        send[z] = get(a, (1 - core) * HALF + z)
        return carry

    lax.fori_loop(0, HALF, emit, 0)


def start_kernel(where, gathered, state_out, slabs, a, b, c, *coefs):
    first = where[0] * SLAB
    clear_edges(a)
    clear_edges(b)
    clear_edges(c)
    build(a, coefs, field(gathered, 1), field(gathered, 2), FINE_STEP)
    for z in range(NZ):
        put(a, z, gathered[z // SLAB, 3, z % SLAB])
    fine(a, b, coefs)
    copy_state(a, c)
    copy_slab(a, first, slabs.at[0])
    fine(a, b, coefs)
    copy_slab(a, first, slabs.at[1])
    rescale(coefs, float(STEPS))
    step(c, b, coefs, finish=lambda z, value: get(a, z) - value)

    copy_out(b, state_out)
    for z in range(NZ):
        put(a, z, gathered[z // SLAB, 3, z % SLAB])
    step(a, b, coefs, finish=lambda z, value: value + (get(c, z) - value))
    copy_slab(b, first, slabs.at[2])
    step(b, a, coefs, finish=lambda z, value: value + state_out[z])
    copy_slab(a, first, slabs.at[3])
    copy_out(a, state_out)


def chain_kernel(counts, halves, *refs):
    where, gathered, state = refs[0], refs[1], refs[2]
    at = 3
    if halves:
        state_other = refs[3]
        at = 4
    segments = refs[at : at + 2 * len(counts)]
    at += 2 * len(counts)
    state_out, picked, late, forcing, sems, a, b = refs[at : at + 7]
    coefs = refs[at + 7 :]
    first = where[0] * SLAB
    core = where[1]
    target = where[2]
    chips = sum(counts)

    def copies(chip):
        done = 0
        found = []
        for number, count in enumerate(counts):
            found.append((done, done + count, segments[2 * number], segments[2 * number + 1]))
            done += count
        return found

    def copy_of(source, q, chip, slot, side):
        parity = jnp.where(side == 0, core, 1 - core)
        half = parity
        real = slot ^ parity
        return pltpu.make_async_copy(
            source.at[q, real],
            forcing.at[2 * chip + slot, pl.ds(half * HALF, HALF)],
            sems.at[2 * chip + slot, side],
        )

    for low, high, own, other in copies(0):

        def launch(chip, carry, low=low, own=own, other=other):
            for slot in range(2):
                copy_of(own, chip - low, chip, slot, 0).start()
                copy_of(other, chip - low, chip, slot, 1).start()
            return carry

        lax.fori_loop(low, high, launch, 0)

    clear_edges(a)
    clear_edges(b)
    build(a, coefs, field(gathered, 1), field(gathered, 2), COARSE_STEP)

    if halves:

        def load(z, carry):
            put(a, core * HALF + z, state[z])
            put(a, (1 - core) * HALF + z, state_other[z])
            return carry

        lax.fori_loop(0, HALF, load, 0)
    else:

        def load(z, carry):
            put(a, z, state[z])
            return carry

        lax.fori_loop(0, NZ, load, 0)

    copy_slab(a, first, picked)

    def advance(src, dst, chip, slot):
        for side in range(2):
            copy_of(segments[0], 0, chip, slot, side).wait()
        index = 2 * chip + slot
        step(src, dst, coefs, finish=lambda z, value: value + forcing[index, z])

        @pl.when(index == target)
        def _():
            copy_slab(dst, first, picked)

    def pair(chip, carry):
        advance(a, b, chip, 0)
        advance(b, a, chip, 1)
        return carry

    lax.fori_loop(0, chips, pair, 0)
    copy_slab(b, first, late)

    if state_out.shape[0] == NZ:
        copy_out(a, state_out)
    else:

        def out(z, carry):
            state_out[z] = get(a, core * HALF + z)
            return carry

        lax.fori_loop(0, HALF, out, 0)


def params():
    return pltpu.CompilerParams(vmem_limit_bytes=VMEM_BYTES)


def cost(steps):
    cells = NZ * NX * NY
    return pl.CostEstimate(flops=18 * cells * steps, bytes_accessed=4 * 10 * cells * steps, transcendentals=0)


VMEM_SPEC = pl.BlockSpec(memory_space=pltpu.VMEM)
SMEM_SPEC = pl.BlockSpec(memory_space=pltpu.SMEM)
ANY_SPEC = pl.BlockSpec(memory_space=pl.ANY)


def f32(*shape):
    return jax.ShapeDtypeStruct(shape, jnp.float32)


def run_fine(where, gathered):
    return pl.pallas_call(
        fine_kernel,
        out_shape=[f32(HALF, *PLANE), f32(HALF, *PLANE), f32(SLAB, *PLANE), f32(SLAB, *PLANE)],
        in_specs=[SMEM_SPEC, VMEM_SPEC],
        out_specs=[VMEM_SPEC] * 4,
        scratch_shapes=scratch_set(),
        compiler_params=params(),
        cost_estimate=cost(18),
    )(where, gathered)


def run_start(where, gathered):
    return pl.pallas_call(
        start_kernel,
        out_shape=[f32(NZ, *PLANE), f32(4, SLAB, *PLANE)],
        in_specs=[SMEM_SPEC, VMEM_SPEC],
        out_specs=[VMEM_SPEC] * 2,
        scratch_shapes=[pltpu.VMEM(PADDED, jnp.float32)] + scratch_set(),
        compiler_params=params(),
        cost_estimate=cost(20),
    )(where, gathered)


def run_chain(where, gathered, states, segments, planes_out):
    counts = tuple(own.shape[0] for own, _ in segments)
    halves = len(states) == 2
    chips = sum(counts)
    arrays = [array for segment in segments for array in segment]
    return pl.pallas_call(
        functools.partial(chain_kernel, counts, halves),
        out_shape=[f32(planes_out, *PLANE), f32(SLAB, *PLANE), f32(SLAB, *PLANE)],
        in_specs=[SMEM_SPEC, VMEM_SPEC] + [VMEM_SPEC] * len(states) + [ANY_SPEC] * len(arrays),
        out_specs=[VMEM_SPEC] * 3,
        scratch_shapes=[
            pltpu.VMEM((2 * chips, NZ, *PLANE), jnp.float32),
            pltpu.SemaphoreType.DMA((2 * chips, 2)),
        ]
        + scratch_set(),
        compiler_params=params(),
        cost_estimate=cost(2 * chips),
    )(where, gathered, *states, *arrays)


def shards(cpoint_guess, initial_state, diffusivity, growth_rate):
    rank = lax.axis_index("tm")
    z_rank = lax.axis_index("gz")
    count = lax.axis_size("tm")
    core = rank % 2
    part = count // 2
    swap = [(i, i ^ 1) for i in range(count)]

    with jax.named_scope("gather_fields"):
        fields = jnp.stack([cpoint_guess[0], diffusivity, growth_rate, initial_state])
        gathered = lax.all_gather(fields, "gz")

    where = jnp.stack([z_rank, core, z_rank]).astype(jnp.int32)
    with jax.named_scope("fine_spans"):
        keep, send, u_slab, w_slab = run_fine(where, gathered)
    with jax.named_scope("forcing_halves"):
        arrived = lax.ppermute(send, "tm", swap)
        mine = jnp.stack([keep, arrived])
    with jax.named_scope("gather_forcing"):
        groups = [[part * g + 2 * q + c for q in range(part // 2)] for g in range(2) for c in range(2)]
        own = lax.all_gather(mine, "tm", axis_index_groups=groups)
    with jax.named_scope("first_intervals"):
        state, slabs = run_start(where, gathered)
    with jax.named_scope("residual"):
        u_prev = lax.ppermute(u_slab, "tm", [(i, i + 1) for i in range(count - 1)])
        w_prev = lax.ppermute(w_slab, "tm", [(i, i + 2) for i in range(count - 2)])
        reached = jnp.where(rank == 0, slabs[0], jnp.where(rank == 1, slabs[1], w_prev))
        relaxed = jnp.where(rank == 0, slabs[0], u_prev)
        residual = reached - relaxed

    lead = 4
    with jax.named_scope("swap_forcing"):
        own_a, own_b = own[:lead], own[lead:]
        other_a = lax.ppermute(own_a, "tm", swap)
        other_b = lax.ppermute(own_b, "tm", swap)

    def where_for(target):
        return jnp.stack([z_rank, core, target]).astype(jnp.int32)

    with jax.named_scope("first_chain"):
        state, picked_a, _ = run_chain(where_for(rank - 2), gathered, [state], [(own_a, other_a)], NZ)
        half, picked_b, late = run_chain(
            where_for(rank - 2 - 2 * lead), gathered, [state], [(own_b, other_b)], HALF
        )
    with jax.named_scope("hand_over"):
        row = 8
        rows = count // row
        pairs = [
            (y * row + i, (rows - 1 - y) * row + i) for y in range(rows // 2) for i in range(row)
        ]
        half = lax.ppermute(half, "tm", pairs)
        other_half = lax.ppermute(half, "tm", swap)
        late = lax.ppermute(late, "tm", [(part - row, part)])
    with jax.named_scope("second_chain"):
        _, picked_c, _ = run_chain(
            where_for(rank - part - 2), gathered, [half, other_half], [(own_a, other_a), (own_b, other_b)], HALF
        )
    with jax.named_scope("corrected"):
        corrected = jnp.where(rank < 2 * lead + 2, picked_a, picked_b)
        corrected = jnp.where(rank == 0, slabs[2], corrected)
        corrected = jnp.where(rank == 1, slabs[3], corrected)
        corrected = jnp.where(rank > part, picked_c, corrected)
        corrected = jnp.where(rank == part, late, corrected)
    return (corrected[None], residual[None])


def solution(mesh):
    in_specs = (
        P("tm", "gz", None, None),
        P("gz", None, None),
        P("gz", None, None),
        P("gz", None, None),
    )
    out_specs = (P("tm", "gz", None, None), P("tm", "gz", None, None))
    return jax.shard_map(shards, mesh=mesh, in_specs=in_specs, out_specs=out_specs, check_vma=False)
```

```python
import functools

import jax
import jax.numpy as jnp
from jax import lax
from jax.experimental import pallas as pl
from jax.experimental.pallas import tpu as pltpu
from jax.sharding import PartitionSpec as P

STEPS = 8
FINE_STEP = 0.01875
COARSE_STEP = FINE_STEP * STEPS
NZ, NX, NY = 32, 32, 128
SLAB = 4
GROUP = 16
ROW = 8
VMEM_BYTES = 48 * 1024 * 1024

PLANE = (NX, NY)
PADDED = (NZ + 2, NX + 16, NY)
MESSAGE = NZ + SLAB


def scratch_set():
    full = pltpu.VMEM((NZ, *PLANE), jnp.float32)
    return [
        pltpu.VMEM(PADDED, jnp.float32),
        pltpu.VMEM(PADDED, jnp.float32),
        pltpu.VMEM((NZ + 1, *PLANE), jnp.float32),
        full,
        full,
        full,
        full,
        full,
        full,
    ]


def put(ref, z, value):
    ref[z + 1, ROW : ROW + NX, :] = value


def get(ref, z):
    return ref[z + 1, ROW : ROW + NX, :]


def clear_edges(ref):
    ref[0] = jnp.zeros(PADDED[1:], jnp.float32)
    ref[NZ + 1] = jnp.zeros(PADDED[1:], jnp.float32)
    for z in range(NZ):
        ref[z + 1, 0:ROW, :] = jnp.zeros((ROW, NY), jnp.float32)
        ref[z + 1, ROW + NX : 2 * ROW + NX, :] = jnp.zeros((ROW, NY), jnp.float32)


def build(a, coefs, kappa, growth, h):
    az, axm, axp, aym, ayp, diag, react = coefs
    half_h = 0.5 * h
    for z in range(NZ):
        put(a, z, kappa(z))
    lane = lax.broadcasted_iota(jnp.int32, PLANE, 1)
    az[0] = half_h * get(a, 0)
    for z in range(NZ):
        k = get(a, z)
        up = half_h * (a[z + 2, ROW : ROW + NX, :] + k)
        down = half_h * (a[z, ROW : ROW + NX, :] + k)
        xm = half_h * (a[z + 1, ROW - 1 : ROW - 1 + NX, :] + k)
        xp = half_h * (a[z + 1, ROW + 1 : ROW + 1 + NX, :] + k)
        ym = half_h * (jnp.where(lane == 0, 0.0, pltpu.roll(k, 1, 1)) + k)
        yp = half_h * (jnp.where(lane == NY - 1, 0.0, pltpu.roll(k, NY - 1, 1)) + k)
        az[z + 1] = up
        axm[z] = xm
        axp[z] = xp
        aym[z] = jnp.where(lane == 0, 0.0, ym)
        ayp[z] = jnp.where(lane == NY - 1, 0.0, yp)
        hr = h * growth(z)
        react[z] = hr
        diag[z] = hr - (up + down + xm + xp + ym + yp)


def step(src, dst, coefs, scale=None, finish=None):
    az, axm, axp, aym, ayp, diag, react = coefs
    below = src[0, ROW : ROW + NX, :]
    here = get(src, 0)
    face = az[0]
    for z in range(NZ):
        above = src[z + 2, ROW : ROW + NX, :]
        next_face = az[z + 1]
        change = here * (diag[z] - react[z] * (here * here))
        change = change + (face * below + next_face * above)
        change = change + (
            axm[z] * src[z + 1, ROW - 1 : ROW - 1 + NX, :]
            + axp[z] * src[z + 1, ROW + 1 : ROW + 1 + NX, :]
        )
        change = change + (aym[z] * pltpu.roll(here, 1, 1) + ayp[z] * pltpu.roll(here, NY - 1, 1))
        if scale is not None:
            change = scale * change
        value = here + change
        if finish is not None:
            value = finish(z, value)
        put(dst, z, value)
        below, here, face = here, above, next_face


def fine(a, b, coefs):
    def pair(i, carry):
        step(a, b, coefs)
        step(b, a, coefs)
        return carry

    lax.fori_loop(0, STEPS // 2, pair, 0)


def copy_slab(src, first, out):
    for i in range(SLAB):
        out[i] = get(src, first + i)


def copy_out(src, out):
    for z in range(NZ):
        out[z] = get(src, z)


def field(gathered, number):
    return lambda z: gathered[z // SLAB, number, z % SLAB]


def fine_kernel(where, gathered, forcing, u_out, w_out, a, b, *coefs):
    first = where[0] * SLAB
    clear_edges(a)
    clear_edges(b)
    build(a, coefs, field(gathered, 1), field(gathered, 2), FINE_STEP)
    for z in range(NZ):
        put(a, z, gathered[z // SLAB, 0, z % SLAB])
    fine(a, b, coefs)
    copy_slab(a, first, u_out)
    step(a, b, coefs, scale=float(STEPS))
    copy_out(b, forcing)
    fine(a, b, coefs)
    copy_slab(a, first, w_out)
    for z in range(NZ):
        forcing[z] = get(a, z) - forcing[z]


def start_kernel(where, gathered, message, slabs, a, b, c, *coefs):
    first = where[0] * SLAB
    clear_edges(a)
    clear_edges(b)
    clear_edges(c)
    build(a, coefs, field(gathered, 1), field(gathered, 2), FINE_STEP)
    for z in range(NZ):
        put(a, z, gathered[z // SLAB, 3, z % SLAB])
    fine(a, b, coefs)
    copy_slab(a, first, slabs.at[0])
    for z in range(NZ):
        put(c, z, get(a, z))
    fine(a, b, coefs)
    copy_slab(a, first, slabs.at[1])
    scale = float(STEPS)
    step(c, b, coefs, scale=scale)
    for z in range(NZ):
        message[z] = get(a, z) - get(b, z)
        put(a, z, gathered[z // SLAB, 3, z % SLAB])
    step(a, b, coefs, scale=scale, finish=lambda z, value: value + (get(c, z) - value))
    for i in range(SLAB):
        message[NZ + i] = get(b, first + i)
    step(b, a, coefs, scale=scale, finish=lambda z, value: value + message[z])
    copy_out(a, message)


def chain_kernel(where, gathered, message, gathered_forcing, message_out, picked, forcing, sems, a, b, *coefs):
    first = where[0] * SLAB
    wanted = where[1]

    def copy_of(index):
        return pltpu.make_async_copy(gathered_forcing.at[index], forcing.at[index], sems.at[index])

    for index in range(GROUP):
        copy_of(index).start()

    clear_edges(a)
    clear_edges(b)
    build(a, coefs, field(gathered, 1), field(gathered, 2), COARSE_STEP)
    for z in range(NZ):
        put(a, z, message[z])

    @pl.when(wanted == 0)
    def _():
        for i in range(SLAB):
            picked[0, i] = message[NZ + i]
            picked[1, i] = get(a, first + i)

    def advance(src, dst, index):
        copy_of(index).wait()
        step(src, dst, coefs, finish=lambda z, value: value + forcing[index, z])

    def pick(src, slot, number):
        for i in range(SLAB):
            picked[slot, i] = get(src, first + i)

    def pair(i, carry):
        advance(a, b, 2 * i)
        advance(b, a, 2 * i + 1)
        number = 2 * i + 2

        @pl.when(number == wanted)
        def _():
            pick(b, 0, number)
            pick(a, 1, number)

        @pl.when(number == wanted + GROUP // 2)
        def _():
            pick(b, 2, number)
            pick(a, 3, number)

        return carry

    lax.fori_loop(0, GROUP // 2, pair, 0)
    copy_out(a, message_out)
    for i in range(SLAB):
        message_out[NZ + i] = get(b, first + i)


def params():
    return pltpu.CompilerParams(vmem_limit_bytes=VMEM_BYTES)


def cost(steps):
    cells = NZ * NX * NY
    return pl.CostEstimate(flops=18 * cells * steps, bytes_accessed=4 * 10 * cells * steps, transcendentals=0)


VMEM_SPEC = pl.BlockSpec(memory_space=pltpu.VMEM)
SMEM_SPEC = pl.BlockSpec(memory_space=pltpu.SMEM)
ANY_SPEC = pl.BlockSpec(memory_space=pl.ANY)


def f32(*shape):
    return jax.ShapeDtypeStruct(shape, jnp.float32)


def run_fine(where, gathered):
    return pl.pallas_call(
        fine_kernel,
        out_shape=[f32(NZ, *PLANE), f32(SLAB, *PLANE), f32(SLAB, *PLANE)],
        in_specs=[SMEM_SPEC, VMEM_SPEC],
        out_specs=[VMEM_SPEC] * 3,
        scratch_shapes=scratch_set(),
        compiler_params=params(),
        cost_estimate=cost(18),
    )(where, gathered)


def run_start(where, gathered):
    return pl.pallas_call(
        start_kernel,
        out_shape=[f32(MESSAGE, *PLANE), f32(2, SLAB, *PLANE)],
        in_specs=[SMEM_SPEC, VMEM_SPEC],
        out_specs=[VMEM_SPEC] * 2,
        scratch_shapes=[pltpu.VMEM(PADDED, jnp.float32)] + scratch_set(),
        compiler_params=params(),
        cost_estimate=cost(20),
    )(where, gathered)


def run_chain(where, gathered, message, forcing):
    return pl.pallas_call(
        chain_kernel,
        out_shape=[f32(MESSAGE, *PLANE), f32(4, SLAB, *PLANE)],
        in_specs=[SMEM_SPEC, VMEM_SPEC, VMEM_SPEC, ANY_SPEC],
        out_specs=[VMEM_SPEC] * 2,
        scratch_shapes=[
            pltpu.VMEM((GROUP, NZ, *PLANE), jnp.float32),
            pltpu.SemaphoreType.DMA((GROUP,)),
        ]
        + scratch_set(),
        compiler_params=params(),
        cost_estimate=cost(GROUP),
    )(where, gathered, message, forcing)


def shards(cpoint_guess, initial_state, diffusivity, growth_rate):
    rank = lax.axis_index("tm")
    z_rank = lax.axis_index("gz")
    count = lax.axis_size("tm")
    groups = count // GROUP
    core = rank % 2
    place = rank % GROUP
    half = GROUP // 2
    where = jnp.stack([z_rank, place]).astype(jnp.int32)

    with jax.named_scope("gather_fields"):
        fields = jnp.stack([cpoint_guess[0], diffusivity, growth_rate, initial_state])
        gathered = lax.all_gather(fields, "gz")
    with jax.named_scope("fine_spans"):
        forcing, u_slab, w_slab = run_fine(where, gathered)
    with jax.named_scope("gather_forcing"):
        members = [[GROUP * g + i for i in range(GROUP)] for g in range(groups)]
        forcing = lax.all_gather(forcing, "tm", axis_index_groups=members)
    with jax.named_scope("first_intervals"):
        message, slabs = run_start(where, gathered)
    with jax.named_scope("residual"):
        u_prev = lax.ppermute(u_slab, "tm", [(i, i + 1) for i in range(count - 1)])
        w_prev = lax.ppermute(w_slab, "tm", [(i, i + 2) for i in range(count - 2)])
        reached = jnp.where(rank == 0, slabs[0], jnp.where(rank == 1, slabs[1], w_prev))
        relaxed = jnp.where(rank == 0, slabs[0], u_prev)
        residual = reached - relaxed
        message, residual = lax.optimization_barrier((message, residual))

    results = None
    for g in range(groups):
        with jax.named_scope("chain"):
            message, picked = run_chain(where, gathered, message, forcing)
        if results is None:
            results = picked
        else:
            results = jnp.where(rank // GROUP == g, picked, results)
        if g + 1 < groups:
            with jax.named_scope("hand_over"):
                hosts = [(GROUP * g + i, GROUP * (g + 1) + i) for i in range(0, half, 2)]
                message = lax.ppermute(message, "tm", hosts)
    with jax.named_scope("spread_results"):
        down = [(i, i + half) for i in range(0, count, 2) if i % GROUP < half]
        pair = lax.ppermute(results[2:], "tm", down)
        pair = jnp.where(place < half, results[:2], pair)
        odd = lax.ppermute(pair[1], "tm", [(i, i + 1) for i in range(0, count, 2)])
        corrected = jnp.where(core == 0, pair[0], odd)
    return (corrected[None], residual[None])


def solution(mesh):
    in_specs = (
        P("tm", "gz", None, None),
        P("gz", None, None),
        P("gz", None, None),
        P("gz", None, None),
    )
    out_specs = (P("tm", "gz", None, None), P("tm", "gz", None, None))
    return jax.shard_map(shards, mesh=mesh, in_specs=in_specs, out_specs=out_specs, check_vma=False)
```

```python
import functools

import jax
import jax.numpy as jnp
from jax import lax
from jax.experimental import pallas as pl
from jax.experimental.pallas import tpu as pltpu
from jax.sharding import PartitionSpec as P

STEPS = 8
FINE_STEP = 0.01875
COARSE_STEP = FINE_STEP * STEPS
NZ, NX, NY = 32, 32, 128
SLAB = 4
SHARE = 2
GROUP = 16
ROW = 8
VMEM_BYTES = 48 * 1024 * 1024

PLANE = (NX, NY)
PADDED = (NZ + 2, NX + 16, NY)
COEFFICIENTS = [(NZ + 1, *PLANE)] + [(NZ, *PLANE)] * 5
MESSAGE = NZ + SLAB


def scratch_set():
    return [pltpu.VMEM(PADDED, jnp.float32)] * 2 + [pltpu.VMEM(shape, jnp.float32) for shape in COEFFICIENTS]


def put(ref, z, value):
    ref[z + 1, ROW : ROW + NX, :] = value


def get(ref, z):
    return ref[z + 1, ROW : ROW + NX, :]


def clear_edges(ref):
    ref[0] = jnp.zeros(PADDED[1:], jnp.float32)
    ref[NZ + 1] = jnp.zeros(PADDED[1:], jnp.float32)
    for z in range(NZ):
        ref[z + 1, 0:ROW, :] = jnp.zeros((ROW, NY), jnp.float32)
        ref[z + 1, ROW + NX : 2 * ROW + NX, :] = jnp.zeros((ROW, NY), jnp.float32)


def build(a, coefs, kappa, growth, h):
    az, ax, aym, ayp, diag, react = coefs
    half_h = 0.5 * h
    for z in range(NZ):
        put(a, z, kappa(z))
    row = lax.broadcasted_iota(jnp.int32, PLANE, 0)
    lane = lax.broadcasted_iota(jnp.int32, PLANE, 1)
    az[0] = half_h * get(a, 0)
    for z in range(NZ):
        k = get(a, z)
        up = half_h * (a[z + 2, ROW : ROW + NX, :] + k)
        down = half_h * (a[z, ROW : ROW + NX, :] + k)
        ym = half_h * (jnp.where(lane == 0, 0.0, pltpu.roll(k, 1, 1)) + k)
        yp = half_h * (jnp.where(lane == NY - 1, 0.0, pltpu.roll(k, NY - 1, 1)) + k)
        ends = jnp.where((row == 0) | (row == NX - 1), half_h * k, 0.0)
        xp = half_h * (a[z + 1, ROW + 1 : ROW + 1 + NX, :] + k)
        az[z + 1] = up
        ax[z] = jnp.where(row == NX - 1, 0.0, xp)
        aym[z] = jnp.where(lane == 0, 0.0, ym)
        ayp[z] = jnp.where(lane == NY - 1, 0.0, yp)
        hr = h * growth(z)
        react[z] = hr
        diag[z] = 1.0 + (hr - (up + down + ends + ym + yp))


def step(src, dst, coefs, scale=None, finish=None):
    az, ax, aym, ayp, diag, react = coefs
    below = src[0, ROW : ROW + NX, :]
    here = get(src, 0)
    face = az[0]
    for z in range(NZ):
        above = src[z + 2, ROW : ROW + NX, :]
        next_face = az[z + 1]
        centre = diag[z] if scale is None else diag[z] - 1.0
        value = here * (centre - react[z] * (here * here))
        value = value + (face * below + next_face * above)
        flux = ax[z] * (src[z + 1, ROW + 1 : ROW + 1 + NX, :] - here)
        value = value + (flux - pltpu.roll(flux, 1, 0))
        value = value + (aym[z] * pltpu.roll(here, 1, 1) + ayp[z] * pltpu.roll(here, NY - 1, 1))
        if scale is not None:
            value = here + scale * value
        if finish is not None:
            value = finish(z, value)
        put(dst, z, value)
        below, here, face = here, above, next_face


def fine(a, b, coefs):
    def pair(i, carry):
        step(a, b, coefs)
        step(b, a, coefs)
        return carry

    lax.fori_loop(0, STEPS // 2, pair, 0)


def copy_slab(src, first, out):
    for i in range(SLAB):
        out[i] = get(src, first + i)


def copy_out(src, out):
    for z in range(NZ):
        out[z] = get(src, z)


def kappa_of(fields):
    return lambda z: fields[z % SLAB, z // SLAB]


def growth_of(fields):
    return lambda z: fields[SLAB + z % SLAB, z // SLAB]


def fine_kernel(where, gathered, piece1, piece2, piece3, forcing, u_out, w_out, fields, a, b, *coefs):
    first = where[0] * SLAB
    quarter = where[2]
    for slab in range(NZ // SLAB):
        for i in range(SHARE):
            fields[SHARE * quarter + i, slab] = gathered[slab, SLAB + i]
            for j, piece in enumerate((piece1, piece2, piece3)):
                fields[SHARE * (quarter ^ (j + 1)) + i, slab] = piece[slab, i]
    clear_edges(a)
    clear_edges(b)
    build(a, coefs, kappa_of(fields), growth_of(fields), FINE_STEP)
    for z in range(NZ):
        put(a, z, gathered[z // SLAB, z % SLAB])
    fine(a, b, coefs)
    copy_slab(a, first, u_out)
    step(a, b, coefs, scale=float(STEPS))
    copy_out(b, forcing)
    fine(a, b, coefs)
    copy_slab(a, first, w_out)
    for z in range(NZ):
        forcing[z] = get(a, z) - forcing[z]


def start_kernel(where, fields, initial, message, slabs, a, b, c, *coefs):
    first = where[0] * SLAB
    clear_edges(a)
    clear_edges(b)
    clear_edges(c)
    build(a, coefs, kappa_of(fields), growth_of(fields), FINE_STEP)
    for z in range(NZ):
        put(a, z, initial[z // SLAB, z % SLAB])
    fine(a, b, coefs)
    copy_slab(a, first, slabs.at[0])
    for z in range(NZ):
        put(c, z, get(a, z))
    fine(a, b, coefs)
    copy_slab(a, first, slabs.at[1])
    scale = float(STEPS)
    step(c, b, coefs, scale=scale)
    for z in range(NZ):
        message[z] = get(a, z) - get(b, z)
        put(a, z, initial[z // SLAB, z % SLAB])
    step(a, b, coefs, scale=scale, finish=lambda z, value: value + (get(c, z) - value))
    for i in range(SLAB):
        message[NZ + i] = get(b, first + i)
    step(b, a, coefs, scale=scale, finish=lambda z, value: value + message[z])
    copy_out(a, message)


def chain_kernel(last, where, fields, message, gathered_forcing, *refs):
    if last:
        picked, forcing, sems, a, b, *coefs = refs
    else:
        message_out, picked, forcing, sems, a, b, *coefs = refs
    first = where[0] * SLAB
    wanted = where[1]

    def copy_of(index):
        return pltpu.make_async_copy(gathered_forcing.at[index], forcing.at[index], sems.at[index])

    for index in range(GROUP):
        copy_of(index).start()

    clear_edges(a)
    clear_edges(b)
    build(a, coefs, kappa_of(fields), growth_of(fields), COARSE_STEP)
    for z in range(NZ):
        put(a, z, message[z])

    @pl.when(wanted == 0)
    def _():
        for i in range(SLAB):
            picked[0, i] = message[NZ + i]
            picked[1, i] = get(a, first + i)

    def advance(src, dst, index):
        copy_of(index).wait()
        step(src, dst, coefs, finish=lambda z, value: value + forcing[index, z])

    def pick(src, slot, number):
        for i in range(SLAB):
            picked[slot, i] = get(src, first + i)

    def pair(i, carry):
        advance(a, b, 2 * i)
        advance(b, a, 2 * i + 1)
        number = 2 * i + 2

        @pl.when(number == wanted)
        def _():
            pick(b, 0, number)
            pick(a, 1, number)

        @pl.when(number == wanted + GROUP // 2)
        def _():
            pick(b, 2, number)
            pick(a, 3, number)

        return carry

    lax.fori_loop(0, GROUP // 2, pair, 0)
    if not last:
        copy_out(a, message_out)
        for i in range(SLAB):
            message_out[NZ + i] = get(b, first + i)


def params():
    return pltpu.CompilerParams(vmem_limit_bytes=VMEM_BYTES)


def cost(steps):
    cells = NZ * NX * NY
    return pl.CostEstimate(flops=18 * cells * steps, bytes_accessed=4 * 10 * cells * steps, transcendentals=0)


VMEM_SPEC = pl.BlockSpec(memory_space=pltpu.VMEM)
SMEM_SPEC = pl.BlockSpec(memory_space=pltpu.SMEM)
ANY_SPEC = pl.BlockSpec(memory_space=pl.ANY)


def f32(*shape):
    return jax.ShapeDtypeStruct(shape, jnp.float32)


def run_fine(where, gathered, pieces):
    return pl.pallas_call(
        fine_kernel,
        out_shape=[
            f32(NZ, *PLANE),
            f32(SLAB, *PLANE),
            f32(SLAB, *PLANE),
            f32(2 * SLAB, NZ // SLAB, *PLANE),
        ],
        in_specs=[SMEM_SPEC] + [VMEM_SPEC] * 4,
        out_specs=[VMEM_SPEC] * 4,
        scratch_shapes=scratch_set(),
        compiler_params=params(),
        cost_estimate=cost(18),
    )(where, gathered, *pieces)


def run_start(where, fields, initial):
    return pl.pallas_call(
        start_kernel,
        out_shape=[f32(MESSAGE, *PLANE), f32(2, SLAB, *PLANE)],
        in_specs=[SMEM_SPEC, VMEM_SPEC, VMEM_SPEC],
        out_specs=[VMEM_SPEC] * 2,
        scratch_shapes=[pltpu.VMEM(PADDED, jnp.float32)] + scratch_set(),
        compiler_params=params(),
        cost_estimate=cost(20),
    )(where, fields, initial)


def run_chain(where, fields, message, forcing, last):
    outs = ([] if last else [f32(MESSAGE, *PLANE)]) + [f32(4, SLAB, *PLANE)]
    return pl.pallas_call(
        functools.partial(chain_kernel, last),
        out_shape=outs,
        in_specs=[SMEM_SPEC, VMEM_SPEC, VMEM_SPEC, ANY_SPEC],
        out_specs=[VMEM_SPEC] * len(outs),
        scratch_shapes=[
            pltpu.VMEM((GROUP, NZ, *PLANE), jnp.float32),
            pltpu.SemaphoreType.DMA((GROUP,)),
        ]
        + scratch_set(),
        compiler_params=params(),
        cost_estimate=cost(GROUP),
    )(where, fields, message, forcing)


def shards(cpoint_guess, initial_state, diffusivity, growth_rate):
    rank = lax.axis_index("tm")
    z_rank = lax.axis_index("gz")
    count = lax.axis_size("tm")
    groups = count // GROUP
    core = rank % 2
    place = rank % GROUP
    half = GROUP // 2
    quarter = rank % 4
    where = jnp.stack([z_rank, place, quarter]).astype(jnp.int32)
    across = [(i, i ^ 2) for i in range(count)]
    swap = [(i, i ^ 1) for i in range(count)]

    with jax.named_scope("gather_fields"):
        low = jnp.where(quarter % 2 == 0, diffusivity[:SHARE], diffusivity[SHARE:])
        high = jnp.where(quarter % 2 == 0, growth_rate[:SHARE], growth_rate[SHARE:])
        share = jnp.where(quarter < 2, low, high)
        gathered = lax.all_gather(jnp.concatenate([cpoint_guess[0], share]), "gz")
    with jax.named_scope("share_coefficients"):
        share = gathered[:, SLAB:]
        piece2 = lax.ppermute(share, "tm", across)
        piece1 = lax.ppermute(share, "tm", swap)
        piece3 = lax.ppermute(piece2, "tm", swap)
    with jax.named_scope("fine_spans"):
        forcing, u_slab, w_slab, fields = run_fine(where, gathered, (piece1, piece2, piece3))
    with jax.named_scope("gather_forcing"):
        members = [[GROUP * g + i for i in range(GROUP)] for g in range(groups)]
        forcing = lax.all_gather(forcing, "tm", axis_index_groups=members)
    with jax.named_scope("first_intervals"):
        initial, u_slab = lax.optimization_barrier((initial_state, u_slab))
        initial = lax.all_gather(initial, "gz")
        message, slabs = run_start(where, fields, initial)
    with jax.named_scope("residual"):
        u_prev = lax.ppermute(u_slab, "tm", [(i, i + 1) for i in range(count - 1)])
        w_prev = lax.ppermute(w_slab, "tm", [(i, i + 2) for i in range(count - 2)])
        reached = jnp.where(rank == 0, slabs[0], jnp.where(rank == 1, slabs[1], w_prev))
        relaxed = jnp.where(rank == 0, slabs[0], u_prev)
        residual = reached - relaxed
        message, residual = lax.optimization_barrier((message, residual))

    results = None
    for g in range(groups):
        with jax.named_scope("chain"):
            *message, picked = run_chain(where, fields, message, forcing, g + 1 == groups)
        if results is None:
            results = picked
        else:
            results = jnp.where(rank // GROUP == g, picked, results)
        if g + 1 < groups:
            with jax.named_scope("hand_over"):
                hosts = [(GROUP * g + i, GROUP * (g + 1) + i) for i in range(0, half, 2)]
                message = lax.ppermute(message[0], "tm", hosts)
    with jax.named_scope("spread_results"):
        down = [(i, i + half) for i in range(0, count, 2) if i % GROUP < half]
        pair = lax.ppermute(results[2:], "tm", down)
        pair = jnp.where(place < half, results[:2], pair)
        odd = lax.ppermute(pair[1], "tm", [(i, i + 1) for i in range(0, count, 2)])
        corrected = jnp.where(core == 0, pair[0], odd)
    return (corrected[None], residual[None])


def solution(mesh):
    in_specs = (
        P("tm", "gz", None, None),
        P("gz", None, None),
        P("gz", None, None),
        P("gz", None, None),
    )
    out_specs = (P("tm", "gz", None, None), P("tm", "gz", None, None))
    return jax.shard_map(shards, mesh=mesh, in_specs=in_specs, out_specs=out_specs, check_vma=False)
```

```python
import functools

import jax
import jax.numpy as jnp
from jax import lax
from jax.experimental import pallas as pl
from jax.experimental.pallas import tpu as pltpu
from jax.sharding import PartitionSpec as P

STEPS = 8
FINE_STEP = 0.01875
COARSE_STEP = FINE_STEP * STEPS
NZ, NX, NY = 32, 32, 128
SLAB = 4
SHARE = 3
GROUP = 16
ROW = 8
VMEM_BYTES = 48 * 1024 * 1024

PLANE = (NX, NY)
PADDED = (NZ + 2, NX + 16, NY)
COEFFICIENTS = [(NZ + 1, *PLANE)] + [(NZ, *PLANE)] * 5
MESSAGE = NZ + SLAB


def scratch_set():
    return [pltpu.VMEM(PADDED, jnp.float32)] * 2 + [pltpu.VMEM(shape, jnp.float32) for shape in COEFFICIENTS]


def put(ref, z, value):
    ref[z + 1, ROW : ROW + NX, :] = value


def get(ref, z):
    return ref[z + 1, ROW : ROW + NX, :]


def clear_edges(ref):
    ref[0] = jnp.zeros(PADDED[1:], jnp.float32)
    ref[NZ + 1] = jnp.zeros(PADDED[1:], jnp.float32)
    for z in range(NZ):
        ref[z + 1, 0:ROW, :] = jnp.zeros((ROW, NY), jnp.float32)
        ref[z + 1, ROW + NX : 2 * ROW + NX, :] = jnp.zeros((ROW, NY), jnp.float32)


def build(a, coefs, kappa, growth, h):
    az, ax, aym, ayp, diag, react = coefs
    half_h = 0.5 * h
    for z in range(NZ):
        put(a, z, kappa(z))
    row = lax.broadcasted_iota(jnp.int32, PLANE, 0)
    lane = lax.broadcasted_iota(jnp.int32, PLANE, 1)
    az[0] = half_h * get(a, 0)
    for z in range(NZ):
        k = get(a, z)
        up = half_h * (a[z + 2, ROW : ROW + NX, :] + k)
        down = half_h * (a[z, ROW : ROW + NX, :] + k)
        ym = half_h * (jnp.where(lane == 0, 0.0, pltpu.roll(k, 1, 1)) + k)
        yp = half_h * (jnp.where(lane == NY - 1, 0.0, pltpu.roll(k, NY - 1, 1)) + k)
        ends = jnp.where((row == 0) | (row == NX - 1), half_h * k, 0.0)
        xp = half_h * (a[z + 1, ROW + 1 : ROW + 1 + NX, :] + k)
        az[z + 1] = up
        ax[z] = jnp.where(row == NX - 1, 0.0, xp)
        aym[z] = jnp.where(lane == 0, 0.0, ym)
        ayp[z] = jnp.where(lane == NY - 1, 0.0, yp)
        hr = h * growth(z)
        react[z] = hr
        diag[z] = 1.0 + (hr - (up + down + ends + ym + yp))


def step(src, dst, coefs, scale=None, finish=None):
    az, ax, aym, ayp, diag, react = coefs
    below = src[0, ROW : ROW + NX, :]
    here = get(src, 0)
    face = az[0]
    for z in range(NZ):
        above = src[z + 2, ROW : ROW + NX, :]
        next_face = az[z + 1]
        centre = diag[z] if scale is None else diag[z] - 1.0
        value = here * (centre - react[z] * (here * here))
        value = value + (face * below + next_face * above)
        flux = ax[z] * (src[z + 1, ROW + 1 : ROW + 1 + NX, :] - here)
        value = value + (flux - pltpu.roll(flux, 1, 0))
        value = value + (aym[z] * pltpu.roll(here, 1, 1) + ayp[z] * pltpu.roll(here, NY - 1, 1))
        if scale is not None:
            value = here + scale * value
        if finish is not None:
            value = finish(z, value)
        put(dst, z, value)
        below, here, face = here, above, next_face


def fine(a, b, coefs):
    def pair(i, carry):
        step(a, b, coefs)
        step(b, a, coefs)
        return carry

    lax.fori_loop(0, STEPS // 2, pair, 0)


def copy_slab(src, first, out):
    for i in range(SLAB):
        out[i] = get(src, first + i)


def copy_out(src, out):
    for z in range(NZ):
        out[z] = get(src, z)


def kappa_of(fields):
    return lambda z: fields[z % SLAB, z // SLAB]


def growth_of(fields):
    return lambda z: fields[SLAB + z % SLAB, z // SLAB]


def fine_kernel(where, gathered, crossed, twin, twin_crossed, forcing, u_out, w_out, fields, a, b, *coefs):
    first = where[0] * SLAB
    core = where[2]
    chip = where[3]
    for slab in range(NZ // SLAB):
        for owner, own, other in ((core, gathered.at[slab, SLAB:], crossed), (1 - core, twin.at[slab], twin_crossed)):
            low, high = 3 * owner + 2, 6 + owner
            fields[3 * owner, slab] = own[0]
            fields[3 * owner + 1, slab] = own[1]
            fields[jnp.where(chip == 0, low, high), slab] = own[2]
            fields[jnp.where(chip == 0, high, low), slab] = other[slab, 0]
    clear_edges(a)
    clear_edges(b)
    build(a, coefs, kappa_of(fields), growth_of(fields), FINE_STEP)
    for z in range(NZ):
        put(a, z, gathered[z // SLAB, z % SLAB])
    fine(a, b, coefs)
    copy_slab(a, first, u_out)
    step(a, b, coefs, scale=float(STEPS))
    copy_out(b, forcing)
    fine(a, b, coefs)
    copy_slab(a, first, w_out)
    for z in range(NZ):
        forcing[z] = get(a, z) - forcing[z]


def start_kernel(where, fields, initial, message, slabs, a, b, c, *coefs):
    first = where[0] * SLAB
    clear_edges(a)
    clear_edges(b)
    clear_edges(c)
    build(a, coefs, kappa_of(fields), growth_of(fields), FINE_STEP)
    for z in range(NZ):
        put(a, z, initial[z // SLAB, z % SLAB])
    fine(a, b, coefs)
    copy_slab(a, first, slabs.at[0])
    for z in range(NZ):
        put(c, z, get(a, z))
    fine(a, b, coefs)
    copy_slab(a, first, slabs.at[1])
    scale = float(STEPS)
    step(c, b, coefs, scale=scale)
    for z in range(NZ):
        message[z] = get(a, z) - get(b, z)
        put(a, z, initial[z // SLAB, z % SLAB])
    step(a, b, coefs, scale=scale, finish=lambda z, value: value + (get(c, z) - value))
    for i in range(SLAB):
        message[NZ + i] = get(b, first + i)
    step(b, a, coefs, scale=scale, finish=lambda z, value: value + message[z])
    copy_out(a, message)


def chain_kernel(last, where, fields, message, gathered_forcing, *refs):
    if last:
        picked, forcing, sems, a, b, *coefs = refs
    else:
        message_out, picked, forcing, sems, a, b, *coefs = refs
    first = where[0] * SLAB
    wanted = where[1]

    def copy_of(index):
        return pltpu.make_async_copy(gathered_forcing.at[index], forcing.at[index], sems.at[index])

    for index in range(GROUP):
        copy_of(index).start()

    clear_edges(a)
    clear_edges(b)
    build(a, coefs, kappa_of(fields), growth_of(fields), COARSE_STEP)
    for z in range(NZ):
        put(a, z, message[z])

    @pl.when(wanted == 0)
    def _():
        for i in range(SLAB):
            picked[0, i] = message[NZ + i]
            picked[1, i] = get(a, first + i)

    def advance(src, dst, index):
        copy_of(index).wait()
        step(src, dst, coefs, finish=lambda z, value: value + forcing[index, z])

    def pick(src, slot, number):
        for i in range(SLAB):
            picked[slot, i] = get(src, first + i)

    def pair(i, carry):
        advance(a, b, 2 * i)
        advance(b, a, 2 * i + 1)
        number = 2 * i + 2

        @pl.when(number == wanted)
        def _():
            pick(b, 0, number)
            pick(a, 1, number)

        @pl.when(number == wanted + GROUP // 2)
        def _():
            pick(b, 2, number)
            pick(a, 3, number)

        return carry

    lax.fori_loop(0, GROUP // 2, pair, 0)
    if not last:
        copy_out(a, message_out)
        for i in range(SLAB):
            message_out[NZ + i] = get(b, first + i)


def params():
    return pltpu.CompilerParams(vmem_limit_bytes=VMEM_BYTES)


def cost(steps):
    cells = NZ * NX * NY
    return pl.CostEstimate(flops=18 * cells * steps, bytes_accessed=4 * 10 * cells * steps, transcendentals=0)


VMEM_SPEC = pl.BlockSpec(memory_space=pltpu.VMEM)
SMEM_SPEC = pl.BlockSpec(memory_space=pltpu.SMEM)
ANY_SPEC = pl.BlockSpec(memory_space=pl.ANY)


def f32(*shape):
    return jax.ShapeDtypeStruct(shape, jnp.float32)


def run_fine(where, gathered, pieces):
    return pl.pallas_call(
        fine_kernel,
        out_shape=[
            f32(NZ, *PLANE),
            f32(SLAB, *PLANE),
            f32(SLAB, *PLANE),
            f32(2 * SLAB, NZ // SLAB, *PLANE),
        ],
        in_specs=[SMEM_SPEC] + [VMEM_SPEC] * 4,
        out_specs=[VMEM_SPEC] * 4,
        scratch_shapes=scratch_set(),
        compiler_params=params(),
        cost_estimate=cost(18),
    )(where, gathered, *pieces)


def run_start(where, fields, initial):
    return pl.pallas_call(
        start_kernel,
        out_shape=[f32(MESSAGE, *PLANE), f32(2, SLAB, *PLANE)],
        in_specs=[SMEM_SPEC, VMEM_SPEC, VMEM_SPEC],
        out_specs=[VMEM_SPEC] * 2,
        scratch_shapes=[pltpu.VMEM(PADDED, jnp.float32)] + scratch_set(),
        compiler_params=params(),
        cost_estimate=cost(20),
    )(where, fields, initial)


def run_chain(where, fields, message, forcing, last):
    outs = ([] if last else [f32(MESSAGE, *PLANE)]) + [f32(4, SLAB, *PLANE)]
    return pl.pallas_call(
        functools.partial(chain_kernel, last),
        out_shape=outs,
        in_specs=[SMEM_SPEC, VMEM_SPEC, VMEM_SPEC, ANY_SPEC],
        out_specs=[VMEM_SPEC] * len(outs),
        scratch_shapes=[
            pltpu.VMEM((GROUP, NZ, *PLANE), jnp.float32),
            pltpu.SemaphoreType.DMA((GROUP,)),
        ]
        + scratch_set(),
        compiler_params=params(),
        cost_estimate=cost(GROUP),
    )(where, fields, message, forcing)


def shards(cpoint_guess, initial_state, diffusivity, growth_rate):
    rank = lax.axis_index("tm")
    z_rank = lax.axis_index("gz")
    count = lax.axis_size("tm")
    groups = count // GROUP
    core = rank % 2
    place = rank % GROUP
    half = GROUP // 2
    chip = rank // 2 % 2
    where = jnp.stack([z_rank, place, core, chip]).astype(jnp.int32)
    across = [(i, i ^ 2) for i in range(count)]
    swap = [(i, i ^ 1) for i in range(count)]

    with jax.named_scope("gather_fields"):
        pair = jnp.where(core == 0, diffusivity[:2], jnp.concatenate([diffusivity[3:], growth_rate[:1]]))
        low = jnp.where(core == 0, diffusivity[2:3], growth_rate[1:2])
        high = jnp.where(core == 0, growth_rate[2:3], growth_rate[3:])
        third = jnp.where(chip == 0, low, high)
        gathered = lax.all_gather(jnp.concatenate([cpoint_guess[0], pair, third]), "gz")
    with jax.named_scope("share_coefficients"):
        crossed = lax.ppermute(gathered[:, SLAB + 2 :], "tm", across)
        twin = lax.ppermute(gathered[:, SLAB:], "tm", swap)
        twin_crossed = lax.ppermute(crossed, "tm", swap)
    with jax.named_scope("fine_spans"):
        forcing, u_slab, w_slab, fields = run_fine(where, gathered, (crossed, twin, twin_crossed))
    with jax.named_scope("gather_forcing"):
        members = [[GROUP * g + i for i in range(GROUP)] for g in range(groups)]
        forcing = lax.all_gather(forcing, "tm", axis_index_groups=members)
    with jax.named_scope("first_intervals"):
        initial, u_slab = lax.optimization_barrier((initial_state, u_slab))
        initial = lax.all_gather(initial, "gz")
        message, slabs = run_start(where, fields, initial)
    with jax.named_scope("residual"):
        u_prev = lax.ppermute(u_slab, "tm", [(i, i + 1) for i in range(count - 1)])
        w_prev = lax.ppermute(w_slab, "tm", [(i, i + 2) for i in range(count - 2)])
        reached = jnp.where(rank == 0, slabs[0], jnp.where(rank == 1, slabs[1], w_prev))
        relaxed = jnp.where(rank == 0, slabs[0], u_prev)
        residual = reached - relaxed
        message, residual = lax.optimization_barrier((message, residual))

    results = None
    for g in range(groups):
        with jax.named_scope("chain"):
            *message, picked = run_chain(where, fields, message, forcing, g + 1 == groups)
        if results is None:
            results = picked
        else:
            results = jnp.where(rank // GROUP == g, picked, results)
        if g + 1 < groups:
            with jax.named_scope("hand_over"):
                hosts = [(GROUP * g + i, GROUP * (g + 1) + i) for i in range(0, half, 2)]
                message = lax.ppermute(message[0], "tm", hosts)
    with jax.named_scope("spread_results"):
        down = [(i, i + half) for i in range(0, count, 2) if i % GROUP < half]
        pair = lax.ppermute(results[2:], "tm", down)
        pair = jnp.where(place < half, results[:2], pair)
        odd = lax.ppermute(pair[1], "tm", [(i, i + 1) for i in range(0, count, 2)])
        corrected = jnp.where(core == 0, pair[0], odd)
    return (corrected[None], residual[None])


def solution(mesh):
    in_specs = (
        P("tm", "gz", None, None),
        P("gz", None, None),
        P("gz", None, None),
        P("gz", None, None),
    )
    out_specs = (P("tm", "gz", None, None), P("tm", "gz", None, None))
    return jax.shard_map(shards, mesh=mesh, in_specs=in_specs, out_specs=out_specs, check_vma=False)
```

```python
import functools

import jax
import jax.numpy as jnp
from jax import lax
from jax.experimental import pallas as pl
from jax.experimental.pallas import tpu as pltpu
from jax.sharding import PartitionSpec as P

STEPS = 8
FINE_STEP = 0.01875
COARSE_STEP = FINE_STEP * STEPS
NZ, NX, NY = 32, 32, 128
SLAB = 4
SHARE = 2
GROUP = 16
ROW = 8
AHEAD = 3
VMEM_BYTES = 48 * 1024 * 1024

PLANE = (NX, NY)
PADDED = (NZ + 2, NX + 16, NY)
COEFFICIENTS = [(NZ + 1, *PLANE)] + [(NZ, *PLANE)] * 5
MESSAGE = NZ + SLAB


def scratch_set():
    return [pltpu.VMEM(PADDED, jnp.float32)] * 2 + [pltpu.VMEM(shape, jnp.float32) for shape in COEFFICIENTS]


def put(ref, z, value):
    ref[z + 1, ROW : ROW + NX, :] = value


def get(ref, z):
    return ref[z + 1, ROW : ROW + NX, :]


def clear_edges(ref):
    ref[0] = jnp.zeros(PADDED[1:], jnp.float32)
    ref[NZ + 1] = jnp.zeros(PADDED[1:], jnp.float32)
    for z in range(NZ):
        ref[z + 1, 0:ROW, :] = jnp.zeros((ROW, NY), jnp.float32)
        ref[z + 1, ROW + NX : 2 * ROW + NX, :] = jnp.zeros((ROW, NY), jnp.float32)


def build(a, coefs, kappa, growth, h):
    az, ax, aym, ayp, diag, react = coefs
    half_h = 0.5 * h
    for z in range(NZ):
        put(a, z, kappa(z))
    row = lax.broadcasted_iota(jnp.int32, PLANE, 0)
    lane = lax.broadcasted_iota(jnp.int32, PLANE, 1)
    az[0] = half_h * get(a, 0)
    for z in range(NZ):
        k = get(a, z)
        up = half_h * (a[z + 2, ROW : ROW + NX, :] + k)
        down = half_h * (a[z, ROW : ROW + NX, :] + k)
        ym = half_h * (jnp.where(lane == 0, 0.0, pltpu.roll(k, 1, 1)) + k)
        yp = half_h * (jnp.where(lane == NY - 1, 0.0, pltpu.roll(k, NY - 1, 1)) + k)
        ends = jnp.where((row == 0) | (row == NX - 1), half_h * k, 0.0)
        xp = half_h * (a[z + 1, ROW + 1 : ROW + 1 + NX, :] + k)
        az[z + 1] = up
        ax[z] = jnp.where(row == NX - 1, 0.0, xp)
        aym[z] = jnp.where(lane == 0, 0.0, ym)
        ayp[z] = jnp.where(lane == NY - 1, 0.0, yp)
        hr = h * growth(z)
        react[z] = hr
        diag[z] = 1.0 + (hr - (up + down + ends + ym + yp))


def step(src, dst, coefs, scale=None, finish=None):
    az, ax, aym, ayp, diag, react = coefs
    below = src[0, ROW : ROW + NX, :]
    here = get(src, 0)
    face = az[0]
    for z in range(NZ):
        above = src[z + 2, ROW : ROW + NX, :]
        next_face = az[z + 1]
        centre = diag[z] if scale is None else diag[z] - 1.0
        value = here * (centre - react[z] * (here * here))
        value = value + (face * below + next_face * above)
        flux = ax[z] * (src[z + 1, ROW + 1 : ROW + 1 + NX, :] - here)
        value = value + (flux - pltpu.roll(flux, 1, 0))
        value = value + (aym[z] * pltpu.roll(here, 1, 1) + ayp[z] * pltpu.roll(here, NY - 1, 1))
        if scale is not None:
            value = here + scale * value
        if finish is not None:
            value = finish(z, value)
        put(dst, z, value)
        below, here, face = here, above, next_face


def fine(a, b, coefs):
    def pair(i, carry):
        step(a, b, coefs)
        step(b, a, coefs)
        return carry

    lax.fori_loop(0, STEPS // 2, pair, 0)


def copy_slab(src, first, out):
    for i in range(SLAB):
        out[i] = get(src, first + i)


def copy_out(src, out):
    for z in range(NZ):
        out[z] = get(src, z)


def kappa_of(fields):
    return lambda z: fields[z % SLAB, z // SLAB]


def growth_of(fields):
    return lambda z: fields[SLAB + z % SLAB, z // SLAB]


def fine_kernel(where, gathered, piece1, piece2, piece3, forcing, u_out, w_out, fields, a, b, *coefs):
    first = where[0] * SLAB
    quarter = where[2]
    for slab in range(NZ // SLAB):
        for i in range(SHARE):
            fields[SHARE * quarter + i, slab] = gathered[slab, SLAB + i]
            for j, piece in enumerate((piece1, piece2, piece3)):
                fields[SHARE * (quarter ^ (j + 1)) + i, slab] = piece[slab, i]
    clear_edges(a)
    clear_edges(b)
    build(a, coefs, kappa_of(fields), growth_of(fields), FINE_STEP)
    for z in range(NZ):
        put(a, z, gathered[z // SLAB, z % SLAB])
    fine(a, b, coefs)
    copy_slab(a, first, u_out)
    step(a, b, coefs, scale=float(STEPS))
    copy_out(b, forcing)
    fine(a, b, coefs)
    copy_slab(a, first, w_out)
    for z in range(NZ):
        forcing[z] = get(a, z) - forcing[z]


def start_kernel(where, fields, initial, message, slabs, a, b, c, *coefs):
    first = where[0] * SLAB
    clear_edges(a)
    clear_edges(b)
    clear_edges(c)
    build(a, coefs, kappa_of(fields), growth_of(fields), FINE_STEP)
    for z in range(NZ):
        put(a, z, initial[z // SLAB, z % SLAB])
    fine(a, b, coefs)
    copy_slab(a, first, slabs.at[0])
    for z in range(NZ):
        put(c, z, get(a, z))
    fine(a, b, coefs)
    copy_slab(a, first, slabs.at[1])
    scale = float(STEPS)
    step(c, b, coefs, scale=scale)
    for z in range(NZ):
        message[z] = get(a, z) - get(b, z)
        put(a, z, initial[z // SLAB, z % SLAB])
    step(a, b, coefs, scale=scale, finish=lambda z, value: value + (get(c, z) - value))
    for i in range(SLAB):
        message[NZ + i] = get(b, first + i)
    step(b, a, coefs, scale=scale, finish=lambda z, value: value + message[z])
    copy_out(a, message)


def chain_kernel(last, where, fields, message, gathered_forcing, *refs):
    if last:
        picked, forcing, sems, a, b, *coefs = refs
    else:
        message_out, picked, forcing, sems, a, b, *coefs = refs
    first = where[0] * SLAB
    wanted = where[1]

    def copy_of(index):
        return pltpu.make_async_copy(gathered_forcing.at[index], forcing.at[index], sems.at[index])

    for index in range(AHEAD):
        copy_of(index).start()

    clear_edges(a)
    clear_edges(b)
    build(a, coefs, kappa_of(fields), growth_of(fields), COARSE_STEP)
    for z in range(NZ):
        put(a, z, message[z])

    @pl.when(wanted == 0)
    def _():
        for i in range(SLAB):
            picked[0, i] = message[NZ + i]
            picked[1, i] = get(a, first + i)

    def advance(src, dst, index):
        @pl.when(index + AHEAD < GROUP)
        def _():
            copy_of(index + AHEAD).start()

        copy_of(index).wait()
        step(src, dst, coefs, finish=lambda z, value: value + forcing[index, z])

    def pick(src, slot, number):
        for i in range(SLAB):
            picked[slot, i] = get(src, first + i)

    def pair(i, carry):
        advance(a, b, 2 * i)
        advance(b, a, 2 * i + 1)
        number = 2 * i + 2

        @pl.when(number == wanted)
        def _():
            pick(b, 0, number)
            pick(a, 1, number)

        @pl.when(number == wanted + GROUP // 2)
        def _():
            pick(b, 2, number)
            pick(a, 3, number)

        return carry

    lax.fori_loop(0, GROUP // 2, pair, 0)
    if not last:
        copy_out(a, message_out)
        for i in range(SLAB):
            message_out[NZ + i] = get(b, first + i)


def params():
    return pltpu.CompilerParams(vmem_limit_bytes=VMEM_BYTES)


def cost(steps):
    cells = NZ * NX * NY
    return pl.CostEstimate(flops=18 * cells * steps, bytes_accessed=4 * 10 * cells * steps, transcendentals=0)


VMEM_SPEC = pl.BlockSpec(memory_space=pltpu.VMEM)
SMEM_SPEC = pl.BlockSpec(memory_space=pltpu.SMEM)
ANY_SPEC = pl.BlockSpec(memory_space=pl.ANY)


def f32(*shape):
    return jax.ShapeDtypeStruct(shape, jnp.float32)


def run_fine(where, gathered, pieces):
    return pl.pallas_call(
        fine_kernel,
        out_shape=[
            f32(NZ, *PLANE),
            f32(SLAB, *PLANE),
            f32(SLAB, *PLANE),
            f32(2 * SLAB, NZ // SLAB, *PLANE),
        ],
        in_specs=[SMEM_SPEC] + [VMEM_SPEC] * 4,
        out_specs=[VMEM_SPEC] * 4,
        scratch_shapes=scratch_set(),
        compiler_params=params(),
        cost_estimate=cost(18),
    )(where, gathered, *pieces)


def run_start(where, fields, initial):
    return pl.pallas_call(
        start_kernel,
        out_shape=[f32(MESSAGE, *PLANE), f32(2, SLAB, *PLANE)],
        in_specs=[SMEM_SPEC, VMEM_SPEC, VMEM_SPEC],
        out_specs=[VMEM_SPEC] * 2,
        scratch_shapes=[pltpu.VMEM(PADDED, jnp.float32)] + scratch_set(),
        compiler_params=params(),
        cost_estimate=cost(20),
    )(where, fields, initial)


def run_chain(where, fields, message, forcing, last):
    outs = ([] if last else [f32(MESSAGE, *PLANE)]) + [f32(4, SLAB, *PLANE)]
    return pl.pallas_call(
        functools.partial(chain_kernel, last),
        out_shape=outs,
        in_specs=[SMEM_SPEC, VMEM_SPEC, VMEM_SPEC, ANY_SPEC],
        out_specs=[VMEM_SPEC] * len(outs),
        scratch_shapes=[
            pltpu.VMEM((GROUP, NZ, *PLANE), jnp.float32),
            pltpu.SemaphoreType.DMA((GROUP,)),
        ]
        + scratch_set(),
        compiler_params=params(),
        cost_estimate=cost(GROUP),
    )(where, fields, message, forcing)


def shards(cpoint_guess, initial_state, diffusivity, growth_rate):
    rank = lax.axis_index("tm")
    z_rank = lax.axis_index("gz")
    count = lax.axis_size("tm")
    groups = count // GROUP
    core = rank % 2
    place = rank % GROUP
    half = GROUP // 2
    quarter = rank % 4
    where = jnp.stack([z_rank, place, quarter]).astype(jnp.int32)
    across = [(i, i ^ 2) for i in range(count)]
    swap = [(i, i ^ 1) for i in range(count)]

    with jax.named_scope("gather_fields"):
        low = jnp.where(quarter % 2 == 0, diffusivity[:SHARE], diffusivity[SHARE:])
        high = jnp.where(quarter % 2 == 0, growth_rate[:SHARE], growth_rate[SHARE:])
        share = jnp.where(quarter < 2, low, high)
        gathered = lax.all_gather(jnp.concatenate([cpoint_guess[0], share]), "gz")
    with jax.named_scope("share_coefficients"):
        share = gathered[:, SLAB:]
        piece2 = lax.ppermute(share, "tm", across)
        piece1 = lax.ppermute(share, "tm", swap)
        piece3 = lax.ppermute(piece2, "tm", swap)
    with jax.named_scope("fine_spans"):
        forcing, u_slab, w_slab, fields = run_fine(where, gathered, (piece1, piece2, piece3))
    with jax.named_scope("gather_forcing"):
        members = [[GROUP * g + i for i in range(GROUP)] for g in range(groups)]
        forcing = lax.all_gather(forcing, "tm", axis_index_groups=members)
    with jax.named_scope("first_intervals"):
        initial, u_slab = lax.optimization_barrier((initial_state, u_slab))
        initial = lax.all_gather(initial, "gz")
        message, slabs = run_start(where, fields, initial)
    with jax.named_scope("residual"):
        u_prev = lax.ppermute(u_slab, "tm", [(i, i + 1) for i in range(count - 1)])
        w_prev = lax.ppermute(w_slab, "tm", [(i, i + 2) for i in range(count - 2)])
        reached = jnp.where(rank == 0, slabs[0], jnp.where(rank == 1, slabs[1], w_prev))
        relaxed = jnp.where(rank == 0, slabs[0], u_prev)
        residual = reached - relaxed
        message, residual = lax.optimization_barrier((message, residual))

    results = None
    for g in range(groups):
        with jax.named_scope("chain"):
            *message, picked = run_chain(where, fields, message, forcing, g + 1 == groups)
        if results is None:
            results = picked
        else:
            results = jnp.where(rank // GROUP == g, picked, results)
        if g + 1 < groups:
            with jax.named_scope("hand_over"):
                hosts = [(GROUP * g + i, GROUP * (g + 1) + i) for i in range(0, half, 2)]
                message = lax.ppermute(message[0], "tm", hosts)
    with jax.named_scope("spread_results"):
        down = [(i, i + half) for i in range(0, count, 2) if i % GROUP < half]
        pair = lax.ppermute(results[2:], "tm", down)
        pair = jnp.where(place < half, results[:2], pair)
        odd = lax.ppermute(pair[1], "tm", [(i, i + 1) for i in range(0, count, 2)])
        corrected = jnp.where(core == 0, pair[0], odd)
    return (corrected[None], residual[None])


def solution(mesh):
    in_specs = (
        P("tm", "gz", None, None),
        P("gz", None, None),
        P("gz", None, None),
        P("gz", None, None),
    )
    out_specs = (P("tm", "gz", None, None), P("tm", "gz", None, None))
    return jax.shard_map(shards, mesh=mesh, in_specs=in_specs, out_specs=out_specs, check_vma=False)
```

```python
import functools

import jax
import jax.numpy as jnp
from jax import lax
from jax.experimental import pallas as pl
from jax.experimental.pallas import tpu as pltpu
from jax.sharding import PartitionSpec as P

STEPS = 8
FINE_STEP = 0.01875
COARSE_STEP = FINE_STEP * STEPS
NZ, NX, NY = 32, 32, 128
SLAB = 4
SHARE = 2
GROUP = 16
ROW = 8
VMEM_BYTES = 48 * 1024 * 1024

PLANE = (NX, NY)
PADDED = (NZ + 2, NX + 16, NY)
COEFFICIENTS = [(NZ + 1, *PLANE)] + [(NZ, *PLANE)] * 5


def scratch_set():
    return [pltpu.VMEM(PADDED, jnp.float32)] * 2 + [pltpu.VMEM(shape, jnp.float32) for shape in COEFFICIENTS]


def put(ref, z, value):
    ref[z + 1, ROW : ROW + NX, :] = value


def get(ref, z):
    return ref[z + 1, ROW : ROW + NX, :]


def clear_edges(ref):
    ref[0] = jnp.zeros(PADDED[1:], jnp.float32)
    ref[NZ + 1] = jnp.zeros(PADDED[1:], jnp.float32)
    for z in range(NZ):
        ref[z + 1, 0:ROW, :] = jnp.zeros((ROW, NY), jnp.float32)
        ref[z + 1, ROW + NX : 2 * ROW + NX, :] = jnp.zeros((ROW, NY), jnp.float32)


def build(a, coefs, kappa, growth, h):
    az, ax, aym, ayp, diag, react = coefs
    half_h = 0.5 * h
    for z in range(NZ):
        put(a, z, kappa(z))
    row = lax.broadcasted_iota(jnp.int32, PLANE, 0)
    lane = lax.broadcasted_iota(jnp.int32, PLANE, 1)
    az[0] = half_h * get(a, 0)
    for z in range(NZ):
        k = get(a, z)
        up = half_h * (a[z + 2, ROW : ROW + NX, :] + k)
        down = half_h * (a[z, ROW : ROW + NX, :] + k)
        ym = half_h * (jnp.where(lane == 0, 0.0, pltpu.roll(k, 1, 1)) + k)
        yp = half_h * (jnp.where(lane == NY - 1, 0.0, pltpu.roll(k, NY - 1, 1)) + k)
        ends = jnp.where((row == 0) | (row == NX - 1), half_h * k, 0.0)
        xp = half_h * (a[z + 1, ROW + 1 : ROW + 1 + NX, :] + k)
        az[z + 1] = up
        ax[z] = jnp.where(row == NX - 1, 0.0, xp)
        aym[z] = jnp.where(lane == 0, 0.0, ym)
        ayp[z] = jnp.where(lane == NY - 1, 0.0, yp)
        hr = h * growth(z)
        react[z] = hr
        diag[z] = 1.0 + (hr - (up + down + ends + ym + yp))


def step(src, dst, coefs, scale=None, finish=None):
    az, ax, aym, ayp, diag, react = coefs
    below = src[0, ROW : ROW + NX, :]
    here = get(src, 0)
    face = az[0]
    for z in range(NZ):
        above = src[z + 2, ROW : ROW + NX, :]
        next_face = az[z + 1]
        centre = diag[z] if scale is None else diag[z] - 1.0
        value = here * (centre - react[z] * (here * here))
        value = value + (face * below + next_face * above)
        flux = ax[z] * (src[z + 1, ROW + 1 : ROW + 1 + NX, :] - here)
        value = value + (flux - pltpu.roll(flux, 1, 0))
        value = value + (aym[z] * pltpu.roll(here, 1, 1) + ayp[z] * pltpu.roll(here, NY - 1, 1))
        if scale is not None:
            value = here + scale * value
        if finish is not None:
            value = finish(z, value)
        put(dst, z, value)
        below, here, face = here, above, next_face


def fine(a, b, coefs):
    def pair(i, carry):
        step(a, b, coefs)
        step(b, a, coefs)
        return carry

    lax.fori_loop(0, STEPS // 2, pair, 0)


def copy_slab(src, first, out):
    for i in range(SLAB):
        out[i] = get(src, first + i)


def copy_out(src, out):
    for z in range(NZ):
        out[z] = get(src, z)


def kappa_of(fields):
    return lambda z: fields[z % SLAB, z // SLAB]


def growth_of(fields):
    return lambda z: fields[SLAB + z % SLAB, z // SLAB]


def fine_kernel(where, gathered, piece1, piece2, piece3, forcing, u_out, w_out, fields, a, b, *coefs):
    first = where[0] * SLAB
    quarter = where[2]
    for slab in range(NZ // SLAB):
        for i in range(SHARE):
            fields[SHARE * quarter + i, slab] = gathered[slab, SLAB + i]
            for j, piece in enumerate((piece1, piece2, piece3)):
                fields[SHARE * (quarter ^ (j + 1)) + i, slab] = piece[slab, i]
    clear_edges(a)
    clear_edges(b)
    build(a, coefs, kappa_of(fields), growth_of(fields), FINE_STEP)
    for z in range(NZ):
        put(a, z, gathered[z // SLAB, z % SLAB])
    fine(a, b, coefs)
    copy_slab(a, first, u_out)
    step(a, b, coefs, scale=float(STEPS))
    copy_out(b, forcing)
    fine(a, b, coefs)
    copy_slab(a, first, w_out)
    for z in range(NZ):
        forcing[z] = get(a, z) - forcing[z]


def start_kernel(where, fields, initial, message, slabs, a, b, c, *coefs):
    first = where[0] * SLAB
    clear_edges(a)
    clear_edges(b)
    clear_edges(c)
    build(a, coefs, kappa_of(fields), growth_of(fields), FINE_STEP)
    for z in range(NZ):
        put(a, z, initial[z // SLAB, z % SLAB])
    fine(a, b, coefs)
    copy_slab(a, first, slabs.at[0])
    for z in range(NZ):
        put(c, z, get(a, z))
    fine(a, b, coefs)
    copy_slab(a, first, slabs.at[1])
    scale = float(STEPS)
    step(c, b, coefs, scale=scale)
    for z in range(NZ):
        message[z] = get(a, z) - get(b, z)
        put(a, z, initial[z // SLAB, z % SLAB])
    step(a, b, coefs, scale=scale, finish=lambda z, value: value + (get(c, z) - value))
    copy_slab(b, first, slabs.at[2])
    step(b, a, coefs, scale=scale, finish=lambda z, value: value + message[z])
    copy_out(a, message)


def chain_kernel(last, where, fields, message, gathered_forcing, *refs):
    if last:
        picked, forcing, sems, a, b, *coefs = refs
    else:
        message_out, late, picked, forcing, sems, a, b, *coefs = refs
    first = where[0] * SLAB
    wanted = where[1]

    def copy_of(index):
        return pltpu.make_async_copy(gathered_forcing.at[index], forcing.at[index], sems.at[index])

    for index in range(GROUP):
        copy_of(index).start()

    clear_edges(a)
    clear_edges(b)
    build(a, coefs, kappa_of(fields), growth_of(fields), COARSE_STEP)
    for z in range(NZ):
        put(a, z, message[z])

    @pl.when(wanted == 0)
    def _():
        for i in range(SLAB):
            picked[1, i] = get(a, first + i)

    def advance(src, dst, index):
        copy_of(index).wait()
        step(src, dst, coefs, finish=lambda z, value: value + forcing[index, z])

    def pick(src, slot, number):
        for i in range(SLAB):
            picked[slot, i] = get(src, first + i)

    def pair(i, carry):
        advance(a, b, 2 * i)
        advance(b, a, 2 * i + 1)
        number = 2 * i + 2

        @pl.when(number == wanted)
        def _():
            pick(b, 0, number)
            pick(a, 1, number)

        @pl.when(number == wanted + GROUP // 2)
        def _():
            pick(b, 2, number)
            pick(a, 3, number)

        return carry

    lax.fori_loop(0, GROUP // 2, pair, 0)
    if not last:
        copy_out(a, message_out)
        copy_slab(b, first, late)


def params():
    return pltpu.CompilerParams(vmem_limit_bytes=VMEM_BYTES)


def cost(steps):
    cells = NZ * NX * NY
    return pl.CostEstimate(flops=18 * cells * steps, bytes_accessed=4 * 10 * cells * steps, transcendentals=0)


VMEM_SPEC = pl.BlockSpec(memory_space=pltpu.VMEM)
SMEM_SPEC = pl.BlockSpec(memory_space=pltpu.SMEM)
ANY_SPEC = pl.BlockSpec(memory_space=pl.ANY)


def f32(*shape):
    return jax.ShapeDtypeStruct(shape, jnp.float32)


def run_fine(where, gathered, pieces):
    return pl.pallas_call(
        fine_kernel,
        out_shape=[
            f32(NZ, *PLANE),
            f32(SLAB, *PLANE),
            f32(SLAB, *PLANE),
            f32(2 * SLAB, NZ // SLAB, *PLANE),
        ],
        in_specs=[SMEM_SPEC] + [VMEM_SPEC] * 4,
        out_specs=[VMEM_SPEC] * 4,
        scratch_shapes=scratch_set(),
        compiler_params=params(),
        cost_estimate=cost(18),
    )(where, gathered, *pieces)


def run_start(where, fields, initial):
    return pl.pallas_call(
        start_kernel,
        out_shape=[f32(NZ, *PLANE), f32(3, SLAB, *PLANE)],
        in_specs=[SMEM_SPEC, VMEM_SPEC, VMEM_SPEC],
        out_specs=[VMEM_SPEC] * 2,
        scratch_shapes=[pltpu.VMEM(PADDED, jnp.float32)] + scratch_set(),
        compiler_params=params(),
        cost_estimate=cost(20),
    )(where, fields, initial)


def run_chain(where, fields, message, forcing, last):
    outs = ([] if last else [f32(NZ, *PLANE), f32(SLAB, *PLANE)]) + [f32(4, SLAB, *PLANE)]
    return pl.pallas_call(
        functools.partial(chain_kernel, last),
        out_shape=outs,
        in_specs=[SMEM_SPEC, VMEM_SPEC, VMEM_SPEC, ANY_SPEC],
        out_specs=[VMEM_SPEC] * len(outs),
        scratch_shapes=[
            pltpu.VMEM((GROUP, NZ, *PLANE), jnp.float32),
            pltpu.SemaphoreType.DMA((GROUP,)),
        ]
        + scratch_set(),
        compiler_params=params(),
        cost_estimate=cost(GROUP),
    )(where, fields, message, forcing)


def shards(cpoint_guess, initial_state, diffusivity, growth_rate):
    rank = lax.axis_index("tm")
    z_rank = lax.axis_index("gz")
    count = lax.axis_size("tm")
    groups = count // GROUP
    core = rank % 2
    place = rank % GROUP
    half = GROUP // 2
    quarter = rank % 4
    where = jnp.stack([z_rank, place, quarter]).astype(jnp.int32)
    across = [(i, i ^ 2) for i in range(count)]
    swap = [(i, i ^ 1) for i in range(count)]

    with jax.named_scope("gather_fields"):
        low = jnp.where(quarter % 2 == 0, diffusivity[:SHARE], diffusivity[SHARE:])
        high = jnp.where(quarter % 2 == 0, growth_rate[:SHARE], growth_rate[SHARE:])
        share = jnp.where(quarter < 2, low, high)
        gathered = lax.all_gather(jnp.concatenate([cpoint_guess[0], share]), "gz")
    with jax.named_scope("share_coefficients"):
        share = gathered[:, SLAB:]
        piece2 = lax.ppermute(share, "tm", across)
        piece1 = lax.ppermute(share, "tm", swap)
        piece3 = lax.ppermute(piece2, "tm", swap)
    with jax.named_scope("fine_spans"):
        forcing, u_slab, w_slab, fields = run_fine(where, gathered, (piece1, piece2, piece3))
    with jax.named_scope("gather_forcing"):
        members = [[GROUP * g + i for i in range(GROUP)] for g in range(groups)]
        forcing = lax.all_gather(forcing, "tm", axis_index_groups=members)
    with jax.named_scope("first_intervals"):
        initial, u_slab = lax.optimization_barrier((initial_state, u_slab))
        initial = lax.all_gather(initial, "gz")
        message, slabs = run_start(where, fields, initial)
    with jax.named_scope("residual"):
        u_prev = lax.ppermute(u_slab, "tm", [(i, i + 1) for i in range(count - 1)])
        w_prev = lax.ppermute(w_slab, "tm", [(i, i + 2) for i in range(count - 2)])
        reached = jnp.where(rank == 0, slabs[0], jnp.where(rank == 1, slabs[1], w_prev))
        relaxed = jnp.where(rank == 0, slabs[0], u_prev)
        residual = reached - relaxed
        message, residual = lax.optimization_barrier((message, residual))

    results = None
    for g in range(groups):
        with jax.named_scope("chain"):
            *message, picked = run_chain(where, fields, message, forcing, g + 1 == groups)
        if results is None:
            results = picked
        else:
            results = jnp.where(rank // GROUP == g, picked, results)
        if g + 1 < groups:
            with jax.named_scope("hand_over"):
                hosts = [(GROUP * g + i, GROUP * (g + 1) + i) for i in range(0, half, 2)]
                late = jnp.where(rank // GROUP == g, message[1], late) if g else message[1]
                message = lax.ppermute(message[0], "tm", hosts)
            if g + 2 == groups:
                with jax.named_scope("late_slabs"):
                    late = lax.ppermute(late, "tm", [(i, i + GROUP) for i in range(0, count - GROUP, GROUP)])
                    late = jnp.where(rank == 0, slabs[2], late)
    with jax.named_scope("spread_results"):
        down = [(i, i + half) for i in range(0, count, 2) if i % GROUP < half]
        pair = lax.ppermute(results[2:], "tm", down)
        pair = jnp.where(place < half, results[:2], pair)
        odd = lax.ppermute(pair[1], "tm", [(i, i + 1) for i in range(0, count, 2)])
        corrected = jnp.where(place == 0, late, jnp.where(core == 0, pair[0], odd))
    return (corrected[None], residual[None])


def solution(mesh):
    in_specs = (
        P("tm", "gz", None, None),
        P("gz", None, None),
        P("gz", None, None),
        P("gz", None, None),
    )
    out_specs = (P("tm", "gz", None, None), P("tm", "gz", None, None))
    return jax.shard_map(shards, mesh=mesh, in_specs=in_specs, out_specs=out_specs, check_vma=False)
```
